32 devices in a mesh: groups: 2 (over y), tok: 8 (over z, x), ch: 2 (over core).
Axes of the slice: x: 2, y: 2, z: 4, core: 2. Of those that a mesh axis runs over, the one named last changes fastest.
Arguments:
- fields: bfloat16 [4096, 512], P(('groups', 'tok'), 'ch'), parts along dimension 0, may hold values from -55 to 55
- cotangent: bfloat16 [4096, 512], P(('groups', 'tok'), 'ch'), parts along dimension 0, may hold values from -6 to 6
- labels: int32 [4096], P(('groups', 'tok')), parts along dimension 0, may hold values from 0 to 511
- reward_masks: int32 [6, 4096], P(None, ('groups', 'tok')), parts along dimension 1, may hold values 0 or 1
- cat_weight: float32 [512], replicated, may hold values from 0.25 to 4
- var_weight: float32 [6], replicated, may hold values from 0.2 to 2
- qkv_weight: bfloat16 [3, 512, 512], P(None, None, 'ch'), may hold values from -0.25 to 0.25
- out_weight: bfloat16 [512, 512], P('ch'), may hold values from -0.25 to 0.25
Outputs:
- grad_fields: bfloat16 [4096, 512], P(('groups', 'tok'), 'ch'), parts along dimension 0
- grad_qkv_weight: float32 [6, 512, 512], P('groups', None, 'ch'), parts along dimension 0
- grad_out_weight: float32 [1024, 512], P(('groups', 'ch')), parts along dimension 0
The draws below stay inside these ranges and needn't reach their ends.
There are 2 independent parts, one for each index of `groups`. The reference program is written for one: setup_inputs(seed, part) draws one part's arguments, and reference() takes and returns one part's arrays. A program takes and returns all parts, laid end to end along the dimension named above; an argument that names none is the same for every part. Nothing has to cross between parts.
All inputs are finite; a program needn't handle non-finite values. No bound on the sum of `reward_masks` on one device may be relied on, other than what follows from the above.
Results may differ from the reference program's by a relative error of at most 0.012.
Values may be sent and summed in bfloat16 or wider, within the bound.
A program may use at most 64 MiB of HBM per device.

```python
import math
import jax
import jax.numpy as jnp
import numpy as np
from jax import lax

D = 512
HEADS = 32
CLASSES = 512
VARIABLES = 6
HEAD_DIM = 16
FIELD_TOKENS = 2048
CELL_TOKENS = 32
N_CH = 2


def draw_fields(key, part):
    key = jax.random.fold_in(key, 11)
    key_standard, key_column = jax.random.split(key, 2)
    standard = jax.random.truncated_normal(key_standard, -4.0, 4.0, (FIELD_TOKENS, D), jnp.float32)
    column = jnp.exp(jax.random.uniform(key_column, (D,), jnp.float32, math.log(0.5), math.log(5.0)))
    return (standard * column).astype(jnp.bfloat16)


def set_ends(values, key, smallest, top_value):
    place = [jax.random.randint(jax.random.fold_in(key, axis), (), 0, length) for axis, length in enumerate(values.shape)]
    widest = values.shape.index(max(values.shape))
    next_to = place[:widest] + [(place[widest] + 1) % values.shape[widest]] + place[widest + 1:]
    return values.at[tuple(place)].set(smallest).at[tuple(next_to)].set(top_value)


def level_of(rng, shape, cuts, low, top_value):
    gain = 1.0
    for dim, shards_of in cuts:
        steps = jax.random.uniform(jax.random.fold_in(jax.random.fold_in(rng, 6), dim), (shards_of,), jnp.float32, low / len(cuts), top_value / len(cuts))
        gain = gain * jnp.repeat(jnp.exp(steps), shape[dim] // shards_of).reshape((-1,) + (1,) * (len(shape) - 1 - dim))
    return gain


def rank_bounds(count, lean):
    loads = [(1 << 20) // math.isqrt(standing ** lean) + 1 for standing in range(1, count + 1)]
    spread = 1 + sum(loads) // (1 << 30)
    return np.cumsum(np.array([max(1, weight // spread) for weight in loads]))


def skewed_ids(stream_key, shape, number_of, skew):
    table = rank_bounds(number_of, skew)
    ticket = jax.random.randint(jax.random.fold_in(stream_key, 1), shape, 0, int(table[number_of - 1]))
    standing = jnp.searchsorted(jnp.asarray(table, jnp.int32), ticket, side="right")
    return jax.random.permutation(jax.random.fold_in(stream_key, 2), number_of)[standing].astype(jnp.int32)


def centred(key, dims, deviation, limit, cuts=(), kind=jnp.bfloat16):
    loudness = level_of(key, dims, cuts, -0.22, 0.18) if cuts else 1.0
    entries = jax.random.normal(key, dims, jnp.float32) * deviation * loudness
    return jnp.minimum(jnp.maximum(entries, -limit), limit).astype(kind)


def setup_inputs(seed: int = 0, part: int = 0) -> dict:
    splits = jax.random.split(jax.random.key(seed), 9)
    part_keys = jax.random.split(jax.random.fold_in(splits[8], part), 9)
    return {
        "fields": draw_fields(jax.random.fold_in(jax.random.fold_in(splits[8], part), 71), part),
        "cotangent": centred(part_keys[1], (FIELD_TOKENS, D), 1.0, 6.0, ((0, 8), (1, 2))),
        "labels": set_ends(skewed_ids(part_keys[2], (FIELD_TOKENS,), CLASSES, 2), jax.random.fold_in(part_keys[2], 3), 0, CLASSES - 1).astype(jnp.int32),
        "reward_masks": set_ends((jax.random.randint(part_keys[3], (VARIABLES, FIELD_TOKENS), 0, 2) < 1).astype(jnp.int32), jax.random.fold_in(part_keys[3], 1), 0, 1),
        "cat_weight": jnp.clip(jnp.exp(jax.random.uniform(splits[4], (CLASSES,), jnp.float32, math.log(0.25), math.log(4.0))), 0.25, 4.0),
        "var_weight": jnp.clip(jnp.exp(jax.random.uniform(splits[5], (VARIABLES,), jnp.float32, math.log(0.2), math.log(2.0))), 0.2, 2.0),
        "qkv_weight": centred(splits[6], (3, D, D), D ** -0.5, 0.25, ((2, 2),)),
        "out_weight": centred(splits[7], (D, D), D ** -0.5, 0.25, ((0, 2),)),
    }


def token_weight(labels, reward_masks, cat_weight, var_weight):
    classes = lax.broadcasted_iota(jnp.int32, (1, cat_weight.shape[0]), 1)
    picked = lax.optimization_barrier(jnp.sum(jnp.where(labels[:, None] == classes, cat_weight[None, :], 0.0), axis=1))
    reward_boost = 1.0 + jnp.einsum('v,vn->n', var_weight, reward_masks.astype(jnp.float32))
    return picked * reward_boost

def group_order(array):
    channels = array.shape[-1]
    shaped = array.reshape(64, CELL_TOKENS, channels)
    return shaped.transpose(1, 0, 2).reshape(-1, channels)

def field_order(array):
    channels = array.shape[-1]
    shaped = array.reshape(CELL_TOKENS, 64, channels)
    return shaped.transpose(1, 0, 2).reshape(-1, channels)

def normalize(field_block):
    values = field_block.astype(jnp.float32)
    centered = values - lax.optimization_barrier(jnp.mean(values, axis=1, keepdims=True))
    inv_std = lax.rsqrt(lax.optimization_barrier(jnp.mean(centered * centered, axis=1, keepdims=True)) + 1e-05)
    return (centered * inv_std, inv_std)

def attend_back(projected, grad_out):
    token_count = projected.shape[0]
    groups = token_count // 64
    softmax_scale = HEAD_DIM ** (-0.5)
    pieces = projected.astype(jnp.float32).reshape(groups, 64, 3, HEADS, HEAD_DIM)
    queries = pieces[:, :, 0]
    key_rows = pieces[:, :, 1]
    value_rows = pieces[:, :, 2]
    grad_heads = grad_out.astype(jnp.float32).reshape(groups, 64, HEADS, HEAD_DIM)
    scores = jnp.einsum('gqhd,gkhd->gqhk', queries, key_rows) * softmax_scale
    exponent = jnp.exp(scores)
    attn_probs = exponent / lax.optimization_barrier(jnp.sum(exponent, axis=3, keepdims=True))
    probs_low = lax.optimization_barrier(attn_probs.astype(jnp.bfloat16)).astype(jnp.float32)
    attended = jnp.einsum('gqhk,gkhd->gqhd', probs_low, value_rows).astype(jnp.bfloat16)
    grad_p = jnp.einsum('gqhd,gkhd->gqhk', grad_heads, value_rows)
    grad_scores = attn_probs * (grad_p - lax.optimization_barrier(jnp.sum(attn_probs * grad_p, axis=3, keepdims=True)))
    grad_low = lax.optimization_barrier(grad_scores.astype(jnp.bfloat16)).astype(jnp.float32)
    grad_q = jnp.einsum('gqhk,gkhd->gqhd', grad_low, key_rows) * softmax_scale
    grad_k = jnp.einsum('gqhk,gqhd->gkhd', grad_low, queries) * softmax_scale
    grad_v = jnp.einsum('gqhk,gqhd->gkhd', probs_low, grad_heads)
    grad_proj = jnp.stack([grad_q, grad_k, grad_v], axis=2).astype(jnp.bfloat16)
    return (attended.reshape(token_count, D), grad_proj.reshape(token_count, 3, D))

def reference(fields, cotangent, labels, reward_masks, cat_weight, var_weight, qkv_weight, out_weight):
    weight = token_weight(labels, reward_masks, cat_weight, var_weight)
    weighted = (cotangent.astype(jnp.float32) * weight[:, None]).astype(jnp.bfloat16)
    all_tokens = FIELD_TOKENS
    block_size = math.gcd(all_tokens, 4096)
    field_blocks = group_order(fields).reshape(-1, block_size, D)
    grad_blocks = group_order(weighted).reshape(-1, block_size, D)
    half_width = D // N_CH

    def accumulate(sums_now, blocks_pair):
        field_block, grad_block = blocks_pair
        unit_fields, inv_std = normalize(field_block)
        normed = unit_fields.astype(jnp.bfloat16)
        projected = jnp.einsum('nc,jcd->njd', normed.astype(jnp.float32), qkv_weight.astype(jnp.float32)).astype(jnp.bfloat16)
        grad_out = jnp.dot(grad_block, out_weight.T, preferred_element_type=jnp.float32).astype(jnp.bfloat16)
        attended, grad_proj = attend_back(projected, grad_out)
        grad_qkv_sum = sums_now[0] + jnp.einsum('nc,njd->jcd', normed.astype(jnp.float32), grad_proj.astype(jnp.float32))
        grad_out_sum = sums_now[1] + jnp.dot(attended.T, grad_block, preferred_element_type=jnp.float32)
        dense_grad = jnp.zeros((block_size, D), jnp.float32)
        for half_index in range(N_CH):
            col_start = half_index * half_width
            partial_value = jnp.einsum('njd,jcd->nc', grad_proj[:, :, col_start:col_start + half_width].astype(jnp.float32), qkv_weight[:, :, col_start:col_start + half_width].astype(jnp.float32))
            partial_value = lax.optimization_barrier(partial_value.astype(jnp.bfloat16))
            dense_grad = dense_grad + partial_value.astype(jnp.float32)
        mean_grad = lax.optimization_barrier(jnp.mean(dense_grad, axis=1, keepdims=True))
        second = lax.optimization_barrier(jnp.mean(dense_grad * unit_fields, axis=1, keepdims=True))
        grad_block_fields = (grad_block.astype(jnp.float32) + inv_std * (dense_grad - mean_grad - unit_fields * second)).astype(jnp.bfloat16)
        return ((grad_qkv_sum, grad_out_sum), grad_block_fields)
    initial = (jnp.zeros((3, D, D), jnp.float32), jnp.zeros((D, D), jnp.float32))
    sums_done, grad_field_blocks = lax.scan(accumulate, initial, (field_blocks, grad_blocks))
    grad_fields = field_order(grad_field_blocks.reshape(all_tokens, D))
    return (grad_fields, sums_done[0], sums_done[1])
```

```python
import functools

import jax
import jax.numpy as jnp
from jax import lax
from jax.experimental import pallas as pl
from jax.experimental.pallas import tpu as pltpu
from jax.sharding import PartitionSpec as P

HEAD_DIM = 16
MEMBERS = 64
F32 = jnp.float32
BF16 = jnp.bfloat16
MESH = pl.DeviceIdType.MESH


def nn(a, b):
    return lax.dot_general(a, b, (((1,), (0,)), ((), ())), preferred_element_type=F32)


def nt(a, b):
    return lax.dot_general(a, b, (((1,), (1,)), ((), ())), preferred_element_type=F32)


def tn(a, b):
    return lax.dot_general(a, b, (((0,), (0,)), ((), ())), preferred_element_type=F32)


def iota(shape, dim):
    return lax.broadcasted_iota(jnp.int32, shape, dim)


def repeat(start, stop, body):
    if stop - start <= 8:
        for k in range(start, stop):
            body(k)
    else:
        lax.fori_loop(start, stop, lambda k, _: (body(k), 0)[1], 0)


def spread_matrix(tokens, spread, rows, slots, transposed):
    shape = (tokens, spread * slots) if transposed else (spread * slots, tokens)
    slot, token = (1, 0) if transposed else (0, 1)
    slot, token = iota(shape, slot), iota(shape, token)
    peer, place = slot // slots, slot % slots
    hit = (token == place * spread + peer) & (place < rows)
    return jnp.where(hit, 1.0, 0.0).astype(BF16)


def group_matrix(tokens, spread, rows, slots, transposed):
    shape = (spread * slots, tokens) if transposed else (tokens, spread * slots)
    token, slot = (1, 0) if transposed else (0, 1)
    token, slot = iota(shape, token), iota(shape, slot)
    groups = tokens // MEMBERS
    source = (token % MEMBERS) * groups + token // MEMBERS
    peer, place = slot // slots, slot % slots
    hit = (source == peer * rows + place) & (place < rows)
    return jnp.where(hit, 1.0, 0.0).astype(BF16)


def split_sum(values, ones):
    high = values.astype(BF16)
    low = (values - high.astype(F32)).astype(BF16)
    return nn(high, ones) + nn(low, ones)


def attend(q, k, v, g):
    channels = q.shape[1]
    per = 256 // MEMBERS
    wide = per * MEMBERS
    scale = HEAD_DIM ** (-0.5)
    row_head = iota((wide, channels), 0) // MEMBERS
    col_head = iota((wide, channels), 1) // HEAD_DIM
    ones = iota((wide, wide), 0) // MEMBERS == iota((wide, wide), 1) // MEMBERS
    ones = jnp.where(ones, 1.0, 0.0).astype(BF16)
    k_all = jnp.concatenate([k] * per, axis=0)
    v_all = jnp.concatenate([v] * per, axis=0)
    attended = grad_q = grad_k = grad_v = None
    for chunk in range(channels // HEAD_DIM // per):
        own = row_head + chunk * per == col_head
        keep = jnp.where(own, 1.0, 0.0).astype(BF16)
        k_wide = k_all * keep
        v_wide = v_all * keep
        exponent = jnp.exp(nt(q, k_wide) * scale)
        probs = exponent / split_sum(exponent, ones)
        low = probs.astype(BF16)
        grad_p = nt(g, v_wide)
        grad_scores = probs * (grad_p - split_sum(probs * grad_p, ones))
        grad_low = grad_scores.astype(BF16)
        terms = [nn(low, v_wide), nn(grad_low, k_wide)]
        for left, right in ((grad_low, q), (low, g)):
            full = jnp.where(own, tn(left, right), 0.0)
            part = full[:MEMBERS]
            for h in range(1, per):
                part = part + full[h * MEMBERS:(h + 1) * MEMBERS]
            terms.append(part)
        if chunk == 0:
            attended, grad_q, grad_k, grad_v = terms
        else:
            attended, grad_q = attended + terms[0], grad_q + terms[1]
            grad_k, grad_v = grad_k + terms[2], grad_v + terms[3]
    return (
        attended.astype(BF16),
        (grad_q * scale).astype(BF16),
        (grad_k * scale).astype(BF16),
        grad_v.astype(BF16),
    )


def kernel(
    spread,
    fields,
    cotangent,
    labels,
    masks,
    cat_weight,
    var_weight,
    qkv_weight,
    out_weight,
    out_fields,
    sums,
    send,
    got,
    dense_send,
    dense_got,
    back_send,
    back_got,
    terms,
    from_x,
    pair,
    from_z,
    stack,
    in_send,
    in_recv,
    fw_send,
    fw_recv,
    de_send,
    de_recv,
    bk_send,
    bk_recv,
    x_send,
    x_recv,
    z_send,
    z_recv,
    gz_send,
    gz_recv,
    gx_send,
    gx_recv,
):
    me = lax.axis_index("tok")
    ch = lax.axis_index("ch")
    x, z = lax.rem(me, 2), me // 2
    partner = 2 * z + 1 - x
    tokens, channels = fields.shape
    rows = tokens // spread
    slots = send.shape[1]
    parts, _, depth, block, _ = terms.shape

    def remote(src, dst, send_sem, recv_sem, where):
        return pltpu.make_async_remote_copy(
            src_ref=src, dst_ref=dst, send_sem=send_sem, recv_sem=recv_sem,
            device_id=where, device_id_type=MESH,
        )

    barrier = pltpu.get_barrier_semaphore()

    def greet(k):
        pl.semaphore_signal(
            barrier, inc=1, device_id={"tok": lax.rem(me + k, spread)}, device_id_type=MESH
        )

    repeat(1, spread, greet)
    pl.semaphore_signal(barrier, inc=1, device_id={"ch": 1 - ch}, device_id_type=MESH)

    classes = cat_weight.shape[1]
    onehot = jnp.where(iota((classes, tokens), 0) == labels[...], 1.0, 0.0).astype(BF16)
    left = jnp.broadcast_to(cat_weight[...], (16, classes))
    picked = jnp.zeros((16, tokens), F32)
    for _ in range(3):
        piece = left.astype(BF16)
        picked = picked + nn(piece, onehot)
        left = left - piece.astype(F32)
    boost = jnp.ones((1, tokens), F32)
    seen = masks[...].astype(F32)
    for variable in range(masks.shape[0]):
        boost = boost + var_weight[variable] * seen[variable:variable + 1]
    weight_row = picked[:1] * boost
    diagonal = iota((tokens, tokens), 0) == iota((tokens, tokens), 1)
    weight = jnp.sum(jnp.where(diagonal, weight_row, 0.0), axis=1, keepdims=True)
    weighted = (cotangent[...].astype(F32) * weight).astype(BF16)
    order = spread_matrix(tokens, spread, rows, slots, False)
    send[:, :, :channels] = nn(order, fields[...]).astype(BF16).reshape(spread, slots, channels)
    send[:, :, channels:] = nn(order, weighted).astype(BF16).reshape(spread, slots, channels)

    pl.semaphore_wait(barrier, spread)

    def to_peer(k):
        peer = lax.rem(me + k, spread)
        return remote(
            send.at[peer], got.at[ch, me], in_send.at[peer], in_recv.at[me], {"tok": peer}
        )

    def from_peer(k):
        peer = lax.rem(me + spread - k, spread)
        return peer, remote(
            send.at[peer], got.at[ch, peer], in_send.at[peer], in_recv.at[peer], {"tok": peer}
        )

    def forward(peer):
        return remote(
            got.at[ch, peer], got.at[ch, peer], fw_send.at[peer], fw_recv.at[peer], {"ch": 1 - ch}
        )

    def sibling(peer):
        return remote(
            got.at[1 - ch, peer], got.at[1 - ch, peer], fw_send.at[peer], fw_recv.at[peer],
            {"ch": 1 - ch},
        )

    repeat(1, spread, lambda k: to_peer(k).start())
    got[ch, me] = send[me]
    forward(me).start()

    def pass_on(k):
        peer, copy = from_peer(k)
        copy.wait_recv()
        forward(peer).start()

    repeat(1, spread, pass_on)
    repeat(0, spread, lambda k: sibling(k).wait_recv())

    place = group_matrix(tokens, spread, rows, slots, False)
    low = nn(place, got[0].reshape(spread * slots, 2 * channels))
    high = nn(place, got[1].reshape(spread * slots, 2 * channels))
    values = jnp.concatenate([low[:, :channels], high[:, :channels]], axis=1)
    grad_full = jnp.concatenate([low[:, channels:], high[:, channels:]], axis=1).astype(BF16)
    centered = values - jnp.mean(values, axis=1, keepdims=True)
    inv_std = lax.rsqrt(jnp.mean(centered * centered, axis=1, keepdims=True) + 1e-05)
    unit = centered * inv_std
    normed = unit.astype(BF16)
    q = nn(normed, qkv_weight[0]).astype(BF16)
    k = nn(normed, qkv_weight[1]).astype(BF16)
    v = nn(normed, qkv_weight[2]).astype(BF16)
    g = nt(grad_full, out_weight[...]).astype(BF16)
    for group in range(tokens // MEMBERS):
        rows_of = slice(group * MEMBERS, (group + 1) * MEMBERS)
        results = attend(q[rows_of], k[rows_of], v[rows_of], g[rows_of])
        for index, result in enumerate(results):
            stack[index, rows_of] = result

    def to_partner(part):
        return remote(
            terms.at[part, 1 - x], from_x.at[part], x_send.at[part], x_recv.at[part],
            {"tok": partner},
        )

    def store_terms(index, value):
        value = value.astype(BF16)
        if parts == 4:
            terms[index] = value.reshape(2, depth, block, 256)
        else:
            half = depth // 2
            first = (index % 2) * half
            terms[0, index // 2, first:first + half] = value.reshape(half, block, 256)

    turned = normed.astype(F32).T.astype(BF16)
    out_term = tn(stack[0], grad_full)
    store_terms(3, jnp.concatenate([out_term[:, :256], out_term[:, 256:]], axis=0))
    if parts == 4:
        to_partner(3).start()
    for index in range(3):
        store_terms(index, nn(turned, stack[1 + index]))
        if parts == 4:
            to_partner(index).start()
    if parts == 1:
        to_partner(0).start()
    sequence = (3, 0, 1, 2) if parts == 4 else (0,)

    dense = nt(stack[1], qkv_weight[0]) + nt(stack[2], qkv_weight[1]) + nt(stack[3], qkv_weight[2])
    dense_send[...] = dense.astype(BF16)
    dense_copy = remote(dense_send, dense_got, de_send, de_recv, {"ch": 1 - ch})
    dense_copy.start()

    def to_z(part, step):
        there = lax.rem(z + step, depth)
        return remote(
            pair.at[part, there], from_z.at[part, z],
            z_send.at[part, there], z_recv.at[part, z], {"tok": 2 * there + x},
        )

    def from_z_peer(part, step):
        there = lax.rem(z + step, depth)
        return there, remote(
            pair.at[part, there], from_z.at[part, there],
            z_send.at[part, there], z_recv.at[part, there], {"tok": 2 * there + x},
        )

    def pair_up(part):
        to_partner(part).wait_recv()
        pair[part] = (terms[part, x].astype(F32) + from_x[part].astype(F32)).astype(BF16)
        repeat(1, depth, lambda step: to_z(part, step).start())

    pair_up(sequence[0])

    dense_copy.wait()
    dense = dense_send[...].astype(F32) + dense_got[...].astype(F32)
    mean = jnp.mean(dense, axis=1, keepdims=True)
    second = jnp.mean(dense * unit, axis=1, keepdims=True)
    first_half = ch == 0
    own_dense = jnp.where(first_half, dense[:, :channels], dense[:, channels:])
    own_unit = jnp.where(first_half, unit[:, :channels], unit[:, channels:])
    own_grad = jnp.where(first_half, low[:, channels:], high[:, channels:])
    grad = (own_grad + inv_std * (own_dense - mean - own_unit * second)).astype(BF16)
    place_back = group_matrix(tokens, spread, rows, slots, True)
    back_send[...] = nn(place_back, grad).astype(BF16).reshape(spread, slots, channels)

    def give_back(k):
        peer = lax.rem(me + k, spread)
        return remote(
            back_send.at[peer], back_got.at[me], bk_send.at[peer], bk_recv.at[me], {"tok": peer}
        )

    def take_back(k):
        peer = lax.rem(me + spread - k, spread)
        return remote(
            back_send.at[peer], back_got.at[peer], bk_send.at[peer], bk_recv.at[peer],
            {"tok": peer},
        )

    repeat(1, spread, lambda k: give_back(k).start())
    back_got[me] = back_send[me]

    for part in sequence[1:]:
        pair_up(part)

    def share_z(part, step):
        there = lax.rem(z + step, depth)
        return remote(
            sums.at[part, x, z], sums.at[part, x, z],
            gz_send.at[part, there], gz_recv.at[part, z], {"tok": 2 * there + x},
        )

    def shared_z(part, step):
        there = lax.rem(z + step, depth)
        return there, remote(
            sums.at[part, x, there], sums.at[part, x, there],
            gz_send.at[part, there], gz_recv.at[part, there], {"tok": 2 * there + x},
        )

    def share_x(part, there):
        return remote(
            sums.at[part, x, there], sums.at[part, x, there],
            gx_send.at[part, there], gx_recv.at[part, there], {"tok": partner},
        )

    def shared_x(part, there):
        return remote(
            sums.at[part, 1 - x, there], sums.at[part, 1 - x, there],
            gx_send.at[part, there], gx_recv.at[part, there], {"tok": partner},
        )

    for part in sequence:
        if depth <= 9:
            total = pair[part, z].astype(F32)
            for step in range(1, depth):
                there, copy = from_z_peer(part, step)
                copy.wait_recv()
                total = total + from_z[part, there].astype(F32)
        else:
            def add(step, total):
                there, copy = from_z_peer(part, step)
                copy.wait_recv()
                return total + from_z[part, there].astype(F32)

            total = lax.fori_loop(1, depth, add, pair[part, z].astype(F32))
        sums[part, x, z] = total.astype(BF16)
        repeat(1, depth, lambda step: share_z(part, step).start())
        share_x(part, z).start()

    repeat(1, spread, lambda k: take_back(k).wait_recv())
    order_back = spread_matrix(tokens, spread, rows, slots, True)
    restored = nn(order_back, back_got[...].reshape(spread * slots, channels))
    out_fields[...] = restored.astype(BF16)

    def go_on(part, step):
        there, copy = shared_z(part, step)
        copy.wait_recv()
        share_x(part, there).start()

    for part in sequence:
        repeat(1, depth, lambda step: go_on(part, step))
    for part in sequence:
        repeat(0, depth, lambda there: shared_x(part, there).wait_recv())

    repeat(1, spread, lambda k: to_peer(k).wait_send())
    repeat(0, spread, lambda k: forward(k).wait_send())
    repeat(1, spread, lambda k: give_back(k).wait_send())
    for part in sequence:
        to_partner(part).wait_send()
        repeat(1, depth, lambda step: to_z(part, step).wait_send())
        repeat(1, depth, lambda step: share_z(part, step).wait_send())
        repeat(0, depth, lambda there: share_x(part, there).wait_send())


def shards(fields, cotangent, labels, reward_masks, cat_weight, var_weight, qkv_weight, out_weight):
    tokens, channels = fields.shape
    spread = lax.axis_size("tok")
    slots = max(tokens // spread, 16)
    depth = spread // 2
    width = qkv_weight.shape[1]
    total = 2048
    parts = 4 if total // (4 * spread) >= 16 else 1
    block = total // (parts * spread)
    vmem = pl.BlockSpec(memory_space=pltpu.VMEM)
    smem = pl.BlockSpec(memory_space=pltpu.SMEM)
    dma = pltpu.SemaphoreType.DMA
    grad_fields, sums = pl.pallas_call(
        functools.partial(kernel, spread),
        out_shape=(
            jax.ShapeDtypeStruct((tokens, channels), BF16),
            jax.ShapeDtypeStruct((parts, 2, depth, block, 256), BF16),
        ),
        in_specs=[vmem] * 5 + [smem] + [vmem] * 2,
        out_specs=(vmem, vmem),
        scratch_shapes=[
            pltpu.VMEM((spread, slots, 2 * channels), BF16),
            pltpu.VMEM((2, spread, slots, 2 * channels), BF16),
            pltpu.VMEM((tokens, width), BF16),
            pltpu.VMEM((tokens, width), BF16),
            pltpu.VMEM((spread, slots, channels), BF16),
            pltpu.VMEM((spread, slots, channels), BF16),
            pltpu.VMEM((parts, 2, depth, block, 256), BF16),
            pltpu.VMEM((parts, depth, block, 256), BF16),
            pltpu.VMEM((parts, depth, block, 256), BF16),
            pltpu.VMEM((parts, depth, block, 256), BF16),
            pltpu.VMEM((4, tokens, channels), BF16),
            dma((spread,)), dma((spread,)),
            dma((spread,)), dma((spread,)),
            dma, dma,
            dma((spread,)), dma((spread,)),
            dma((parts,)), dma((parts,)),
            dma((parts, depth)), dma((parts, depth)),
            dma((parts, depth)), dma((parts, depth)),
            dma((parts, depth)), dma((parts, depth)),
        ],
        compiler_params=pltpu.CompilerParams(
            collective_id=0, has_side_effects=True, vmem_limit_bytes=48 * 1024 * 1024
        ),
        cost_estimate=pl.CostEstimate(
            flops=2_000_000_000, bytes_accessed=8_000_000, transcendentals=300_000
        ),
    )(
        fields,
        cotangent,
        labels.reshape(1, tokens),
        reward_masks,
        cat_weight.reshape(1, -1),
        var_weight,
        qkv_weight,
        out_weight,
    )
    sums = sums.reshape(4, 512, 256)
    grad_qkv = sums[:3].astype(F32)
    grad_out = jnp.concatenate([sums[3, :256], sums[3, 256:]], axis=1).astype(F32)
    return grad_fields, grad_qkv, grad_out


def solution(mesh):
    return jax.shard_map(
        shards,
        mesh=mesh,
        in_specs=(
            P(("groups", "tok"), "ch"),
            P(("groups", "tok"), "ch"),
            P(("groups", "tok")),
            P(None, ("groups", "tok")),
            P(),
            P(),
            P(None, None, "ch"),
            P("ch", None),
        ),
        out_specs=(P(("groups", "tok"), "ch"), P("groups", None, "ch"), P(("groups", "ch"), None)),
        check_vma=False,
    )
```

```python
import functools

import jax
import jax.numpy as jnp
from jax import lax
from jax.experimental import pallas as pl
from jax.experimental.pallas import tpu as pltpu
from jax.sharding import PartitionSpec as P

HEAD_DIM = 16
MEMBERS = 64
F32 = jnp.float32
BF16 = jnp.bfloat16
MESH = pl.DeviceIdType.MESH


def nn(a, b):
    return lax.dot_general(a, b, (((1,), (0,)), ((), ())), preferred_element_type=F32)


def nt(a, b):
    return lax.dot_general(a, b, (((1,), (1,)), ((), ())), preferred_element_type=F32)


def tn(a, b):
    return lax.dot_general(a, b, (((0,), (0,)), ((), ())), preferred_element_type=F32)


def iota(shape, dim):
    return lax.broadcasted_iota(jnp.int32, shape, dim)


def repeat(start, stop, body):
    if stop - start <= 8:
        for k in range(start, stop):
            body(k)
    else:
        lax.fori_loop(start, stop, lambda k, _: (body(k), 0)[1], 0)


def spread_matrix(tokens, spread, rows, slots, transposed):
    shape = (tokens, spread * slots) if transposed else (spread * slots, tokens)
    slot, token = (1, 0) if transposed else (0, 1)
    slot, token = iota(shape, slot), iota(shape, token)
    peer, place = slot // slots, slot % slots
    hit = (token == place * spread + peer) & (place < rows)
    return jnp.where(hit, 1.0, 0.0).astype(BF16)


def group_matrix(tokens, spread, rows, slots, transposed):
    shape = (spread * slots, tokens) if transposed else (tokens, spread * slots)
    token, slot = (1, 0) if transposed else (0, 1)
    token, slot = iota(shape, token), iota(shape, slot)
    groups = tokens // MEMBERS
    source = (token % MEMBERS) * groups + token // MEMBERS
    peer, place = slot // slots, slot % slots
    hit = (source == peer * rows + place) & (place < rows)
    return jnp.where(hit, 1.0, 0.0).astype(BF16)


def split_sum(values, ones):
    high = values.astype(BF16)
    low = (values - high.astype(F32)).astype(BF16)
    return nn(high, ones) + nn(low, ones)


def attend(q, k, v, g):
    channels = q.shape[1]
    per = 256 // MEMBERS
    wide = per * MEMBERS
    scale = HEAD_DIM ** (-0.5)
    row_head = iota((wide, channels), 0) // MEMBERS
    col_head = iota((wide, channels), 1) // HEAD_DIM
    ones = iota((wide, wide), 0) // MEMBERS == iota((wide, wide), 1) // MEMBERS
    ones = jnp.where(ones, 1.0, 0.0).astype(BF16)
    k_all = jnp.concatenate([k] * per, axis=0)
    v_all = jnp.concatenate([v] * per, axis=0)
    attended = grad_q = grad_k = grad_v = None
    for chunk in range(channels // HEAD_DIM // per):
        own = row_head + chunk * per == col_head
        keep = jnp.where(own, 1.0, 0.0).astype(BF16)
        k_wide = k_all * keep
        v_wide = v_all * keep
        exponent = jnp.exp(nt(q, k_wide) * scale)
        probs = exponent / split_sum(exponent, ones)
        low = probs.astype(BF16)
        grad_p = nt(g, v_wide)
        grad_scores = probs * (grad_p - split_sum(probs * grad_p, ones))
        grad_low = grad_scores.astype(BF16)
        terms = [nn(low, v_wide), nn(grad_low, k_wide)]
        for left, right in ((grad_low, q), (low, g)):
            full = jnp.where(own, tn(left, right), 0.0)
            part = full[:MEMBERS]
            for h in range(1, per):
                part = part + full[h * MEMBERS:(h + 1) * MEMBERS]
            terms.append(part)
        if chunk == 0:
            attended, grad_q, grad_k, grad_v = terms
        else:
            attended, grad_q = attended + terms[0], grad_q + terms[1]
            grad_k, grad_v = grad_k + terms[2], grad_v + terms[3]
    return (
        attended.astype(BF16),
        (grad_q * scale).astype(BF16),
        (grad_k * scale).astype(BF16),
        grad_v.astype(BF16),
    )


def kernel(
    spread,
    fields_hbm,
    cotangent_hbm,
    labels_hbm,
    masks_hbm,
    cat_weight_hbm,
    var_weight,
    qkv_weight_hbm,
    out_weight_hbm,
    out_fields,
    out_qkv,
    out_out,
    sums,
    fields,
    cotangent,
    labels,
    masks,
    cat_weight,
    qkv_weight,
    out_weight,
    load_sem,
    send,
    got,
    dense_send,
    dense_got,
    back_send,
    back_got,
    terms,
    from_x,
    pair,
    from_z,
    stack,
    in_send,
    in_recv,
    fw_send,
    fw_recv,
    de_send,
    de_recv,
    bk_send,
    bk_recv,
    x_send,
    x_recv,
    z_send,
    z_recv,
    gz_send,
    gz_recv,
    gx_send,
    gx_recv,
):
    loads = [
        pltpu.make_async_copy(source, target, load_sem.at[index])
        for index, (source, target) in enumerate((
            (labels_hbm, labels),
            (cat_weight_hbm, cat_weight),
            (masks_hbm, masks),
            (fields_hbm, fields),
            (cotangent_hbm, cotangent),
            (qkv_weight_hbm, qkv_weight),
            (out_weight_hbm, out_weight),
        ))
    ]
    for load in loads:
        load.start()
    me = lax.axis_index("tok")
    ch = lax.axis_index("ch")
    x, z = lax.rem(me, 2), me // 2
    partner = 2 * z + 1 - x
    tokens, channels = fields.shape
    rows = tokens // spread
    slots = send.shape[1]
    parts, _, depth, block, _ = terms.shape

    def remote(src, dst, send_sem, recv_sem, where):
        return pltpu.make_async_remote_copy(
            src_ref=src, dst_ref=dst, send_sem=send_sem, recv_sem=recv_sem,
            device_id=where, device_id_type=MESH,
        )

    barrier = pltpu.get_barrier_semaphore()

    def greet(k):
        pl.semaphore_signal(
            barrier, inc=1, device_id={"tok": lax.rem(me + k, spread)}, device_id_type=MESH
        )

    repeat(1, spread, greet)
    pl.semaphore_signal(barrier, inc=1, device_id={"ch": 1 - ch}, device_id_type=MESH)

    for load in loads[:5]:
        load.wait()
    classes = cat_weight.shape[1]
    onehot = jnp.where(iota((classes, tokens), 0) == labels[...], 1.0, 0.0).astype(BF16)
    left = jnp.broadcast_to(cat_weight[...], (16, classes))
    picked = jnp.zeros((16, tokens), F32)
    for _ in range(3):
        piece = left.astype(BF16)
        picked = picked + nn(piece, onehot)
        left = left - piece.astype(F32)
    boost = jnp.ones((1, tokens), F32)
    seen = masks[...].astype(F32)
    for variable in range(masks.shape[0]):
        boost = boost + var_weight[variable] * seen[variable:variable + 1]
    weight_row = picked[:1] * boost
    diagonal = iota((tokens, tokens), 0) == iota((tokens, tokens), 1)
    weight = jnp.sum(jnp.where(diagonal, weight_row, 0.0), axis=1, keepdims=True)
    weighted = (cotangent[...].astype(F32) * weight).astype(BF16)
    order = spread_matrix(tokens, spread, rows, slots, False)
    send[:, :, :channels] = nn(order, fields[...]).astype(BF16).reshape(spread, slots, channels)
    send[:, :, channels:] = nn(order, weighted).astype(BF16).reshape(spread, slots, channels)

    pl.semaphore_wait(barrier, spread)

    def to_peer(k):
        peer = lax.rem(me + k, spread)
        return remote(
            send.at[peer], got.at[ch, me], in_send.at[peer], in_recv.at[me], {"tok": peer}
        )

    def from_peer(k):
        peer = lax.rem(me + spread - k, spread)
        return peer, remote(
            send.at[peer], got.at[ch, peer], in_send.at[peer], in_recv.at[peer], {"tok": peer}
        )

    def forward(peer):
        return remote(
            got.at[ch, peer], got.at[ch, peer], fw_send.at[peer], fw_recv.at[peer], {"ch": 1 - ch}
        )

    def sibling(peer):
        return remote(
            got.at[1 - ch, peer], got.at[1 - ch, peer], fw_send.at[peer], fw_recv.at[peer],
            {"ch": 1 - ch},
        )

    repeat(1, spread, lambda k: to_peer(k).start())
    got[ch, me] = send[me]
    forward(me).start()

    def pass_on(k):
        peer, copy = from_peer(k)
        copy.wait_recv()
        forward(peer).start()

    repeat(1, spread, pass_on)
    repeat(0, spread, lambda k: sibling(k).wait_recv())

    for load in loads[5:]:
        load.wait()
    place = group_matrix(tokens, spread, rows, slots, False)
    low = nn(place, got[0].reshape(spread * slots, 2 * channels))
    high = nn(place, got[1].reshape(spread * slots, 2 * channels))
    values = jnp.concatenate([low[:, :channels], high[:, :channels]], axis=1)
    grad_full = jnp.concatenate([low[:, channels:], high[:, channels:]], axis=1).astype(BF16)
    centered = values - jnp.mean(values, axis=1, keepdims=True)
    inv_std = lax.rsqrt(jnp.mean(centered * centered, axis=1, keepdims=True) + 1e-05)
    unit = centered * inv_std
    normed = unit.astype(BF16)
    q = nn(normed, qkv_weight[0]).astype(BF16)
    k = nn(normed, qkv_weight[1]).astype(BF16)
    v = nn(normed, qkv_weight[2]).astype(BF16)
    g = nt(grad_full, out_weight[...]).astype(BF16)
    def to_partner(part):
        return remote(
            terms.at[part, 1 - x], from_x.at[part], x_send.at[part], x_recv.at[part],
            {"tok": partner},
        )

    def store_terms(index, value):
        value = value.astype(BF16)
        if parts == 4:
            terms[index] = value.reshape(2, depth, block, 256)
        else:
            half = depth // 2
            first = (index % 2) * half
            terms[0, index // 2, first:first + half] = value.reshape(half, block, 256)

    def part_rows(ref, index):
        if parts == 4:
            return ref[index].reshape(512, 256)
        first = (index % 2) * (depth // 2)
        return ref[0, index // 2, first:first + depth // 2].reshape(512, 256)

    def to_z(part, step):
        there = lax.rem(z + step, depth)
        return remote(
            pair.at[part, there], from_z.at[part, z],
            z_send.at[part, there], z_recv.at[part, z], {"tok": 2 * there + x},
        )

    def from_z_peer(part, step):
        there = lax.rem(z + step, depth)
        return there, remote(
            pair.at[part, there], from_z.at[part, there],
            z_send.at[part, there], z_recv.at[part, there], {"tok": 2 * there + x},
        )

    def pair_up(part):
        to_partner(part).wait_recv()
        pair[part] = (terms[part, x].astype(F32) + from_x[part].astype(F32)).astype(BF16)
        repeat(1, depth, lambda step: to_z(part, step).start())

    turned = normed.astype(F32).T.astype(BF16)
    groups = tokens // MEMBERS
    half = channels // 2
    for h in range(2):
        cols = slice(h * half, (h + 1) * half)
        for group in range(groups):
            rows_of = slice(group * MEMBERS, (group + 1) * MEMBERS)
            results = attend(
                q[rows_of, cols], k[rows_of, cols], v[rows_of, cols], g[rows_of, cols]
            )
            for index, result in enumerate(results):
                stack[index, rows_of, cols] = result
            if h == 1 and parts == 4 and group == groups - 2:
                pair_up(0)
        both = jnp.concatenate([stack[1, :, cols], stack[2, :, cols]], axis=1)
        store_terms(2 * h, nn(turned, both))
        if parts == 4:
            to_partner(2 * h).start()
        out_term = tn(stack[0, :, cols], grad_full)
        out_term = jnp.concatenate(
            [out_term[:, j * half:(j + 1) * half] for j in range(4)], axis=0
        )
        value_term = nn(turned, stack[3, :, cols])
        store_terms(2 * h + 1, jnp.concatenate([value_term, out_term], axis=1))
        if parts == 4:
            to_partner(2 * h + 1).start()
    if parts == 1:
        to_partner(0).start()

    dense = nt(stack[1], qkv_weight[0]) + nt(stack[2], qkv_weight[1]) + nt(stack[3], qkv_weight[2])
    dense_send[...] = dense.astype(BF16)
    dense_copy = remote(dense_send, dense_got, de_send, de_recv, {"ch": 1 - ch})
    dense_copy.start()

    pair_up(1 if parts == 4 else 0)

    dense_copy.wait()
    dense = dense_send[...].astype(F32) + dense_got[...].astype(F32)
    mean = jnp.mean(dense, axis=1, keepdims=True)
    second = jnp.mean(dense * unit, axis=1, keepdims=True)
    first_half = ch == 0
    own_dense = jnp.where(first_half, dense[:, :channels], dense[:, channels:])
    own_unit = jnp.where(first_half, unit[:, :channels], unit[:, channels:])
    own_grad = jnp.where(first_half, low[:, channels:], high[:, channels:])
    grad = (own_grad + inv_std * (own_dense - mean - own_unit * second)).astype(BF16)
    place_back = group_matrix(tokens, spread, rows, slots, True)
    back_send[...] = nn(place_back, grad).astype(BF16).reshape(spread, slots, channels)

    def give_back(k):
        peer = lax.rem(me + k, spread)
        return remote(
            back_send.at[peer], back_got.at[me], bk_send.at[peer], bk_recv.at[me], {"tok": peer}
        )

    def take_back(k):
        peer = lax.rem(me + spread - k, spread)
        return remote(
            back_send.at[peer], back_got.at[peer], bk_send.at[peer], bk_recv.at[peer],
            {"tok": peer},
        )

    repeat(1, spread, lambda k: give_back(k).start())
    back_got[me] = back_send[me]

    def share_z(part, step):
        there = lax.rem(z + step, depth)
        return remote(
            sums.at[part, x, z], sums.at[part, x, z],
            gz_send.at[part, there], gz_recv.at[part, z], {"tok": 2 * there + x},
        )

    def shared_z(part, step):
        there = lax.rem(z + step, depth)
        return there, remote(
            sums.at[part, x, there], sums.at[part, x, there],
            gz_send.at[part, there], gz_recv.at[part, there], {"tok": 2 * there + x},
        )

    def share_x(part, there):
        return remote(
            sums.at[part, x, there], sums.at[part, x, there],
            gx_send.at[part, there], gx_recv.at[part, there], {"tok": partner},
        )

    def shared_x(part, there):
        return remote(
            sums.at[part, 1 - x, there], sums.at[part, 1 - x, there],
            gx_send.at[part, there], gx_recv.at[part, there], {"tok": partner},
        )

    def go_on(part, step):
        there, copy = shared_z(part, step)
        copy.wait_recv()
        share_x(part, there).start()

    def finish(part):
        if depth <= 9:
            total = pair[part, z].astype(F32)
            for step in range(1, depth):
                there, copy = from_z_peer(part, step)
                copy.wait_recv()
                total = total + from_z[part, there].astype(F32)
        else:
            def add(step, total):
                there, copy = from_z_peer(part, step)
                copy.wait_recv()
                return total + from_z[part, there].astype(F32)

            total = lax.fori_loop(1, depth, add, pair[part, z].astype(F32))
        sums[part, x, z] = total.astype(BF16)
        repeat(1, depth, lambda step: share_z(part, step).start())
        share_x(part, z).start()

    def restore():
        repeat(1, spread, lambda k: take_back(k).wait_recv())
        order_back = spread_matrix(tokens, spread, rows, slots, True)
        restored = nn(order_back, back_got[...].reshape(spread * slots, channels))
        out_fields[...] = restored.astype(BF16)

    def pass_over(part):
        repeat(1, depth, lambda step: go_on(part, step))

    def place_terms(index):
        block_rows = part_rows(sums, index)
        h = index // 2
        cols = slice(h * half, (h + 1) * half)
        if index % 2 == 0:
            out_qkv[0, :, cols] = block_rows[:, :half]
            out_qkv[1, :, cols] = block_rows[:, half:]
        else:
            out_qkv[2, :, cols] = block_rows[:, :half]
            for j in range(4):
                out_out[cols, j * half:(j + 1) * half] = block_rows[j * half:(j + 1) * half, half:]

    if parts == 4:
        finish(0)
        pair_up(2)
        finish(1)
        pass_over(0)
        pair_up(3)
        finish(2)
        pass_over(1)
        restore()
        finish(3)
        pass_over(2)
        pass_over(3)
    else:
        finish(0)
        restore()
        pass_over(0)
    for part in range(parts):
        repeat(0, depth, lambda there: shared_x(part, there).wait_recv())
        if parts == 4:
            place_terms(part)
    if parts == 1:
        for index in range(4):
            place_terms(index)

    repeat(1, spread, lambda k: to_peer(k).wait_send())
    repeat(0, spread, lambda k: forward(k).wait_send())
    repeat(1, spread, lambda k: give_back(k).wait_send())
    for part in range(parts):
        to_partner(part).wait_send()
        repeat(1, depth, lambda step: to_z(part, step).wait_send())
        repeat(1, depth, lambda step: share_z(part, step).wait_send())
        repeat(0, depth, lambda there: share_x(part, there).wait_send())


def shards(fields, cotangent, labels, reward_masks, cat_weight, var_weight, qkv_weight, out_weight):
    tokens, channels = fields.shape
    spread = lax.axis_size("tok")
    slots = max(tokens // spread, 16)
    depth = spread // 2
    width = qkv_weight.shape[1]
    total = 2048
    parts = 4 if total // (4 * spread) >= 16 else 1
    block = total // (parts * spread)
    vmem = pl.BlockSpec(memory_space=pltpu.VMEM)
    hbm = pl.BlockSpec(memory_space=pltpu.HBM)
    smem = pl.BlockSpec(memory_space=pltpu.SMEM)
    dma = pltpu.SemaphoreType.DMA
    grad_fields, grad_qkv, grad_out = pl.pallas_call(
        functools.partial(kernel, spread),
        out_shape=(
            jax.ShapeDtypeStruct((tokens, channels), BF16),
            jax.ShapeDtypeStruct(qkv_weight.shape, BF16),
            jax.ShapeDtypeStruct(out_weight.shape, BF16),
        ),
        in_specs=[hbm] * 5 + [smem] + [hbm] * 2,
        out_specs=(vmem, vmem, vmem),
        scratch_shapes=[
            pltpu.VMEM((parts, 2, depth, block, 256), BF16),
            pltpu.VMEM(fields.shape, BF16),
            pltpu.VMEM(cotangent.shape, BF16),
            pltpu.VMEM((1, tokens), jnp.int32),
            pltpu.VMEM(reward_masks.shape, jnp.int32),
            pltpu.VMEM((1, cat_weight.shape[0]), F32),
            pltpu.VMEM(qkv_weight.shape, BF16),
            pltpu.VMEM(out_weight.shape, BF16),
            dma((7,)),
            pltpu.VMEM((spread, slots, 2 * channels), BF16),
            pltpu.VMEM((2, spread, slots, 2 * channels), BF16),
            pltpu.VMEM((tokens, width), BF16),
            pltpu.VMEM((tokens, width), BF16),
            pltpu.VMEM((spread, slots, channels), BF16),
            pltpu.VMEM((spread, slots, channels), BF16),
            pltpu.VMEM((parts, 2, depth, block, 256), BF16),
            pltpu.VMEM((parts, depth, block, 256), BF16),
            pltpu.VMEM((parts, depth, block, 256), BF16),
            pltpu.VMEM((parts, depth, block, 256), BF16),
            pltpu.VMEM((4, tokens, channels), BF16),
            dma((spread,)), dma((spread,)),
            dma((spread,)), dma((spread,)),
            dma, dma,
            dma((spread,)), dma((spread,)),
            dma((parts,)), dma((parts,)),
            dma((parts, depth)), dma((parts, depth)),
            dma((parts, depth)), dma((parts, depth)),
            dma((parts, depth)), dma((parts, depth)),
        ],
        compiler_params=pltpu.CompilerParams(
            collective_id=0, has_side_effects=True, vmem_limit_bytes=63 * 1024 * 1024
        ),
        cost_estimate=pl.CostEstimate(
            flops=2_000_000_000, bytes_accessed=8_000_000, transcendentals=300_000
        ),
    )(
        fields,
        cotangent,
        labels.reshape(1, tokens),
        reward_masks,
        cat_weight.reshape(1, -1),
        var_weight,
        qkv_weight,
        out_weight,
    )
    return grad_fields, grad_qkv.astype(F32), grad_out.astype(F32)


def solution(mesh):
    return jax.shard_map(
        shards,
        mesh=mesh,
        in_specs=(
            P(("groups", "tok"), "ch"),
            P(("groups", "tok"), "ch"),
            P(("groups", "tok")),
            P(None, ("groups", "tok")),
            P(),
            P(),
            P(None, None, "ch"),
            P("ch", None),
        ),
        out_specs=(P(("groups", "tok"), "ch"), P("groups", None, "ch"), P(("groups", "ch"), None)),
        check_vma=False,
    )
```

```python
import functools

import jax
import jax.numpy as jnp
from jax import lax
from jax.experimental import pallas as pl
from jax.experimental.pallas import tpu as pltpu
from jax.sharding import PartitionSpec as P

HEAD_DIM = 16
MEMBERS = 64
F32 = jnp.float32
BF16 = jnp.bfloat16
MESH = pl.DeviceIdType.MESH


def nn(a, b):
    return lax.dot_general(a, b, (((1,), (0,)), ((), ())), preferred_element_type=F32)


def nt(a, b):
    return lax.dot_general(a, b, (((1,), (1,)), ((), ())), preferred_element_type=F32)


def tn(a, b):
    return lax.dot_general(a, b, (((0,), (0,)), ((), ())), preferred_element_type=F32)


def iota(shape, dim):
    return lax.broadcasted_iota(jnp.int32, shape, dim)


def repeat(start, stop, body):
    if stop - start <= 8:
        for k in range(start, stop):
            body(k)
    else:
        lax.fori_loop(start, stop, lambda k, _: (body(k), 0)[1], 0)


def spread_matrix(tokens, spread, rows, slots, transposed):
    shape = (tokens, spread * slots) if transposed else (spread * slots, tokens)
    slot, token = (1, 0) if transposed else (0, 1)
    slot, token = iota(shape, slot), iota(shape, token)
    peer, place = slot // slots, slot % slots
    hit = (token == place * spread + peer) & (place < rows)
    return jnp.where(hit, 1.0, 0.0).astype(BF16)


def group_matrix(tokens, spread, rows, slots, transposed):
    shape = (spread * slots, tokens) if transposed else (tokens, spread * slots)
    token, slot = (1, 0) if transposed else (0, 1)
    token, slot = iota(shape, token), iota(shape, slot)
    groups = tokens // MEMBERS
    source = (token % MEMBERS) * groups + token // MEMBERS
    peer, place = slot // slots, slot % slots
    hit = (source == peer * rows + place) & (place < rows)
    return jnp.where(hit, 1.0, 0.0).astype(BF16)


def split_sum(values, ones):
    high = values.astype(BF16)
    low = (values - high.astype(F32)).astype(BF16)
    rows = values.shape[0]
    both = nn(jnp.concatenate([high, low], axis=0), ones)
    return both[:rows] + both[rows:]


def attend(q, k, v, g):
    channels = q.shape[1]
    per = 256 // MEMBERS
    wide = per * MEMBERS
    scale = HEAD_DIM ** (-0.5)
    row_head = iota((wide, channels), 0) // MEMBERS
    col_head = iota((wide, channels), 1) // HEAD_DIM
    ones = iota((wide, wide), 0) // MEMBERS == iota((wide, wide), 1) // MEMBERS
    ones = jnp.where(ones, 1.0, 0.0).astype(BF16)
    k_all = jnp.concatenate([k] * per, axis=0)
    v_all = jnp.concatenate([v] * per, axis=0)
    attended = grad_q = grad_k = grad_v = None
    for chunk in range(channels // HEAD_DIM // per):
        own = row_head + chunk * per == col_head
        keep = jnp.where(own, 1.0, 0.0).astype(BF16)
        k_wide = k_all * keep
        v_wide = v_all * keep
        exponent = jnp.exp(nt(q, k_wide) * scale)
        probs = exponent / split_sum(exponent, ones)
        low = probs.astype(BF16)
        grad_p = nt(g, v_wide)
        grad_scores = probs * (grad_p - split_sum(probs * grad_p, ones))
        grad_low = grad_scores.astype(BF16)
        terms = [nn(low, v_wide), nn(grad_low, k_wide)]
        for left, right in ((grad_low, q), (low, g)):
            full = jnp.where(own, tn(left, right), 0.0)
            part = full[:MEMBERS]
            for h in range(1, per):
                part = part + full[h * MEMBERS:(h + 1) * MEMBERS]
            terms.append(part)
        if chunk == 0:
            attended, grad_q, grad_k, grad_v = terms
        else:
            attended, grad_q = attended + terms[0], grad_q + terms[1]
            grad_k, grad_v = grad_k + terms[2], grad_v + terms[3]
    return (
        attended.astype(BF16),
        (grad_q * scale).astype(BF16),
        (grad_k * scale).astype(BF16),
        grad_v.astype(BF16),
    )


def kernel(
    spread,
    fields_hbm,
    cotangent_hbm,
    labels_hbm,
    masks_hbm,
    cat_weight_hbm,
    var_weight,
    qkv_weight_hbm,
    out_weight_hbm,
    out_fields,
    out_qkv,
    out_out,
    sums,
    fields,
    cotangent,
    labels,
    masks,
    cat_weight,
    qkv_weight,
    out_weight,
    load_sem,
    send,
    got,
    dense_send,
    dense_got,
    back_send,
    back_got,
    terms,
    from_x,
    pair,
    from_w,
    quad,
    from_z,
    stack,
    in_send,
    in_recv,
    fw_send,
    fw_recv,
    de_send,
    de_recv,
    bk_send,
    bk_recv,
    x_send,
    x_recv,
    w_send,
    w_recv,
    z_send,
    z_recv,
    gz_send,
    gz_recv,
    gw_send,
    gw_recv,
    gx_send,
    gx_recv,
):
    loads = [
        pltpu.make_async_copy(source, target, load_sem.at[index])
        for index, (source, target) in enumerate((
            (labels_hbm, labels),
            (cat_weight_hbm, cat_weight),
            (masks_hbm, masks),
            (fields_hbm, fields),
            (cotangent_hbm, cotangent),
            (qkv_weight_hbm, qkv_weight),
            (out_weight_hbm, out_weight),
        ))
    ]
    for load in loads:
        load.start()
    me = lax.axis_index("tok")
    ch = lax.axis_index("ch")
    x, z = lax.rem(me, 2), me // 2
    partner = 2 * z + 1 - x
    zl, zh = lax.rem(z, 2), z // 2
    beside = 2 * (2 * zh + 1 - zl) + x
    tokens, channels = fields.shape
    rows = tokens // spread
    slots = send.shape[1]
    parts, _, _, depth, block, _ = terms.shape

    def remote(src, dst, send_sem, recv_sem, where):
        return pltpu.make_async_remote_copy(
            src_ref=src, dst_ref=dst, send_sem=send_sem, recv_sem=recv_sem,
            device_id=where, device_id_type=MESH,
        )

    barrier = pltpu.get_barrier_semaphore()

    def greet(k):
        pl.semaphore_signal(
            barrier, inc=1, device_id={"tok": lax.rem(me + k, spread)}, device_id_type=MESH
        )

    repeat(1, spread, greet)
    pl.semaphore_signal(barrier, inc=1, device_id={"ch": 1 - ch}, device_id_type=MESH)

    for load in loads[:5]:
        load.wait()
    classes = cat_weight.shape[1]
    onehot = jnp.where(iota((classes, tokens), 0) == labels[...], 1.0, 0.0).astype(BF16)
    left = jnp.broadcast_to(cat_weight[...], (16, classes))
    picked = jnp.zeros((16, tokens), F32)
    for _ in range(3):
        piece = left.astype(BF16)
        picked = picked + nn(piece, onehot)
        left = left - piece.astype(F32)
    boost = jnp.ones((1, tokens), F32)
    seen = masks[...].astype(F32)
    for variable in range(masks.shape[0]):
        boost = boost + var_weight[variable] * seen[variable:variable + 1]
    weight_row = picked[:1] * boost
    diagonal = iota((tokens, tokens), 0) == iota((tokens, tokens), 1)
    weight = jnp.sum(jnp.where(diagonal, weight_row, 0.0), axis=1, keepdims=True)
    weighted = (cotangent[...].astype(F32) * weight).astype(BF16)
    order = spread_matrix(tokens, spread, rows, slots, False)
    send[:, :, :channels] = nn(order, fields[...]).astype(BF16).reshape(spread, slots, channels)
    send[:, :, channels:] = nn(order, weighted).astype(BF16).reshape(spread, slots, channels)

    pl.semaphore_wait(barrier, spread)

    def to_peer(k):
        peer = lax.rem(me + k, spread)
        return remote(
            send.at[peer], got.at[ch, me], in_send.at[peer], in_recv.at[me], {"tok": peer}
        )

    def from_peer(k):
        peer = lax.rem(me + spread - k, spread)
        return peer, remote(
            send.at[peer], got.at[ch, peer], in_send.at[peer], in_recv.at[peer], {"tok": peer}
        )

    def forward(peer):
        return remote(
            got.at[ch, peer], got.at[ch, peer], fw_send.at[peer], fw_recv.at[peer], {"ch": 1 - ch}
        )

    def sibling(peer):
        return remote(
            got.at[1 - ch, peer], got.at[1 - ch, peer], fw_send.at[peer], fw_recv.at[peer],
            {"ch": 1 - ch},
        )

    repeat(1, spread, lambda k: to_peer(k).start())
    got[ch, me] = send[me]
    forward(me).start()

    def pass_on(k):
        peer, copy = from_peer(k)
        copy.wait_recv()
        forward(peer).start()

    repeat(1, spread, pass_on)
    repeat(0, spread, lambda k: sibling(k).wait_recv())

    for load in loads[5:]:
        load.wait()
    place = group_matrix(tokens, spread, rows, slots, False)
    low = nn(place, got[0].reshape(spread * slots, 2 * channels))
    high = nn(place, got[1].reshape(spread * slots, 2 * channels))
    values = jnp.concatenate([low[:, :channels], high[:, :channels]], axis=1)
    grad_full = jnp.concatenate([low[:, channels:], high[:, channels:]], axis=1).astype(BF16)
    centered = values - jnp.mean(values, axis=1, keepdims=True)
    inv_std = lax.rsqrt(jnp.mean(centered * centered, axis=1, keepdims=True) + 1e-05)
    unit = centered * inv_std
    normed = unit.astype(BF16)
    q = nn(normed, qkv_weight[0]).astype(BF16)
    k = nn(normed, qkv_weight[1]).astype(BF16)
    v = nn(normed, qkv_weight[2]).astype(BF16)
    g = nt(grad_full, out_weight[...]).astype(BF16)
    def to_partner(part):
        return remote(
            terms.at[part, 1 - x], from_x.at[part], x_send.at[part], x_recv.at[part],
            {"tok": partner},
        )

    def store_terms(index, value):
        value = value.astype(BF16)
        if parts == 4:
            terms[index] = value.reshape(2, 2, depth, block, 256)
        else:
            terms[0, index // 2, index % 2] = value.reshape(depth, block, 256)

    def part_rows(ref, index):
        if parts == 4:
            return ref[index].reshape(512, 256)
        return ref[0, index // 2, index % 2].reshape(512, 256)

    def to_beside(part):
        return remote(
            pair.at[part, 1 - zl], from_w.at[part], w_send.at[part], w_recv.at[part],
            {"tok": beside},
        )

    def z_peer(step):
        there = lax.rem(zh + step, depth)
        return there, {"tok": 2 * (2 * there + zl) + x}

    def to_z(part, step):
        there, where = z_peer(step)
        return remote(
            quad.at[part, there], from_z.at[part, zh],
            z_send.at[part, there], z_recv.at[part, zh], where,
        )

    def from_z_peer(part, step):
        there, where = z_peer(step)
        return there, remote(
            quad.at[part, there], from_z.at[part, there],
            z_send.at[part, there], z_recv.at[part, there], where,
        )

    def pair_up(part):
        to_partner(part).wait_recv()
        pair[part] = (terms[part, x].astype(F32) + from_x[part].astype(F32)).astype(BF16)
        to_beside(part).start()

    def quad_up(part):
        to_beside(part).wait_recv()
        quad[part] = (pair[part, zl].astype(F32) + from_w[part].astype(F32)).astype(BF16)
        repeat(1, depth, lambda step: to_z(part, step).start())

    turned = normed.astype(F32).T.astype(BF16)
    groups = tokens // MEMBERS
    half = channels // 2
    for h in range(2):
        cols = slice(h * half, (h + 1) * half)
        for group in range(groups):
            rows_of = slice(group * MEMBERS, (group + 1) * MEMBERS)
            results = attend(
                q[rows_of, cols], k[rows_of, cols], v[rows_of, cols], g[rows_of, cols]
            )
            for index, result in enumerate(results):
                stack[index, rows_of, cols] = result
            if h == 1 and parts == 4 and group == groups - 2:
                pair_up(0)
        both = jnp.concatenate([stack[1, :, cols], stack[2, :, cols]], axis=1)
        store_terms(2 * h, nn(turned, both))
        if parts == 4:
            to_partner(2 * h).start()
        out_term = tn(stack[0, :, cols], grad_full)
        out_term = jnp.concatenate(
            [out_term[:, j * half:(j + 1) * half] for j in range(4)], axis=0
        )
        value_term = nn(turned, stack[3, :, cols])
        store_terms(2 * h + 1, jnp.concatenate([value_term, out_term], axis=1))
        if parts == 4:
            to_partner(2 * h + 1).start()
    if parts == 1:
        to_partner(0).start()

    dense = nt(stack[1], qkv_weight[0]) + nt(stack[2], qkv_weight[1]) + nt(stack[3], qkv_weight[2])
    dense_send[...] = dense.astype(BF16)
    dense_copy = remote(dense_send, dense_got, de_send, de_recv, {"ch": 1 - ch})
    dense_copy.start()

    if parts == 4:
        quad_up(0)
        pair_up(1)
    else:
        pair_up(0)

    dense_copy.wait()
    dense = dense_send[...].astype(F32) + dense_got[...].astype(F32)
    mean = jnp.mean(dense, axis=1, keepdims=True)
    second = jnp.mean(dense * unit, axis=1, keepdims=True)
    first_half = ch == 0
    own_dense = jnp.where(first_half, dense[:, :channels], dense[:, channels:])
    own_unit = jnp.where(first_half, unit[:, :channels], unit[:, channels:])
    own_grad = jnp.where(first_half, low[:, channels:], high[:, channels:])
    grad = (own_grad + inv_std * (own_dense - mean - own_unit * second)).astype(BF16)
    place_back = group_matrix(tokens, spread, rows, slots, True)
    back_send[...] = nn(place_back, grad).astype(BF16).reshape(spread, slots, channels)

    def give_back(k):
        peer = lax.rem(me + k, spread)
        return remote(
            back_send.at[peer], back_got.at[me], bk_send.at[peer], bk_recv.at[me], {"tok": peer}
        )

    def take_back(k):
        peer = lax.rem(me + spread - k, spread)
        return remote(
            back_send.at[peer], back_got.at[peer], bk_send.at[peer], bk_recv.at[peer],
            {"tok": peer},
        )

    repeat(1, spread, lambda k: give_back(k).start())
    back_got[me] = back_send[me]

    def share_z(part, step):
        there, where = z_peer(step)
        mine = sums.at[part, x, zl, zh]
        return remote(mine, mine, gz_send.at[part, there], gz_recv.at[part, zh], where)

    def shared_z(part, step):
        there, where = z_peer(step)
        other = sums.at[part, x, zl, there]
        return there, remote(
            other, other, gz_send.at[part, there], gz_recv.at[part, there], where
        )

    def share_w(part, there, low_z):
        held = sums.at[part, x, low_z, there]
        return remote(
            held, held, gw_send.at[part, there], gw_recv.at[part, there], {"tok": beside}
        )

    def share_x(part, there, low_z, of_x):
        held = sums.at[part, of_x, low_z, there]
        return remote(
            held, held, gx_send.at[part, low_z, there], gx_recv.at[part, low_z, there],
            {"tok": partner},
        )

    def finish(part):
        if depth <= 9:
            total = quad[part, zh].astype(F32)
            for step in range(1, depth):
                there, copy = from_z_peer(part, step)
                copy.wait_recv()
                total = total + from_z[part, there].astype(F32)
        else:
            def add(step, total):
                there, copy = from_z_peer(part, step)
                copy.wait_recv()
                return total + from_z[part, there].astype(F32)

            total = lax.fori_loop(1, depth, add, quad[part, zh].astype(F32))
        sums[part, x, zl, zh] = total.astype(BF16)
        repeat(1, depth, lambda step: share_z(part, step).start())
        share_w(part, zh, zl).start()
        share_x(part, zh, zl, x).start()

    def go_z(part):
        def go_on(step):
            there, copy = shared_z(part, step)
            copy.wait_recv()
            share_w(part, there, zl).start()
            share_x(part, there, zl, x).start()

        repeat(1, depth, go_on)

    def go_w(part):
        def go_on(step):
            there = lax.rem(zh + step, depth)
            share_w(part, there, 1 - zl).wait_recv()
            share_x(part, there, 1 - zl, x).start()

        repeat(0, depth, go_on)

    def restore():
        repeat(1, spread, lambda k: take_back(k).wait_recv())
        order_back = spread_matrix(tokens, spread, rows, slots, True)
        restored = nn(order_back, back_got[...].reshape(spread * slots, channels))
        out_fields[...] = restored.astype(BF16)

    def place_terms(index):
        block_rows = part_rows(sums, index)
        h = index // 2
        cols = slice(h * half, (h + 1) * half)
        if index % 2 == 0:
            out_qkv[0, :, cols] = block_rows[:, :half]
            out_qkv[1, :, cols] = block_rows[:, half:]
        else:
            out_qkv[2, :, cols] = block_rows[:, :half]
            for j in range(4):
                out_out[cols, j * half:(j + 1) * half] = block_rows[j * half:(j + 1) * half, half:]

    if parts == 4:
        quad_up(1)
        pair_up(2)
        finish(0)
        quad_up(2)
        pair_up(3)
        finish(1)
        go_z(0)
        quad_up(3)
        finish(2)
        go_w(0)
        go_z(1)
        finish(3)
        go_w(1)
        go_z(2)
        restore()
        go_z(3)
        go_w(2)
        go_w(3)
    else:
        quad_up(0)
        finish(0)
        restore()
        go_z(0)
        go_w(0)
    for part in range(parts):
        for low_z in range(2):
            repeat(0, depth, lambda there: share_x(part, there, low_z, 1 - x).wait_recv())
        if parts == 4:
            place_terms(part)
    if parts == 1:
        for index in range(4):
            place_terms(index)

    repeat(1, spread, lambda k: to_peer(k).wait_send())
    repeat(0, spread, lambda k: forward(k).wait_send())
    repeat(1, spread, lambda k: give_back(k).wait_send())
    for part in range(parts):
        to_partner(part).wait_send()
        to_beside(part).wait_send()
        repeat(1, depth, lambda step: to_z(part, step).wait_send())
        repeat(1, depth, lambda step: share_z(part, step).wait_send())
        repeat(0, depth, lambda there: share_w(part, there, zl).wait_send())
        for low_z in range(2):
            repeat(0, depth, lambda there: share_x(part, there, low_z, x).wait_send())


def widen_kernel(fields, qkv, out, fields_wide, qkv_wide, out_wide):
    fields_wide[...] = fields[...]
    qkv_wide[...] = qkv[...].astype(F32)
    out_wide[...] = out[...].astype(F32)


def widen(fields, qkv, out):
    steps = 1
    flat = qkv.reshape(-1, qkv.shape[2])
    arrays = (fields, flat, out)
    specs = [pl.BlockSpec((a.shape[0] // steps, a.shape[1]), lambda i: (i, 0)) for a in arrays]
    fields, flat, out = pl.pallas_call(
        widen_kernel,
        grid=(steps,),
        out_shape=(
            jax.ShapeDtypeStruct(fields.shape, BF16),
            jax.ShapeDtypeStruct(flat.shape, F32),
            jax.ShapeDtypeStruct(out.shape, F32),
        ),
        in_specs=specs,
        out_specs=specs,
        compiler_params=pltpu.CompilerParams(vmem_limit_bytes=63 * 1024 * 1024),
    )(*arrays)
    return fields, flat.reshape(qkv.shape), out


def shards(fields, cotangent, labels, reward_masks, cat_weight, var_weight, qkv_weight, out_weight):
    tokens, channels = fields.shape
    spread = lax.axis_size("tok")
    slots = max(tokens // spread, 16)
    depth = spread // 4
    width = qkv_weight.shape[1]
    total = 2048
    parts = 4 if total // (4 * spread) >= 16 else 1
    block = total // (parts * spread)
    vmem = pl.BlockSpec(memory_space=pltpu.VMEM)
    hbm = pl.BlockSpec(memory_space=pltpu.HBM)
    smem = pl.BlockSpec(memory_space=pltpu.SMEM)
    dma = pltpu.SemaphoreType.DMA
    grad_fields, grad_qkv, grad_out = pl.pallas_call(
        functools.partial(kernel, spread),
        out_shape=(
            jax.ShapeDtypeStruct((tokens, channels), BF16),
            jax.ShapeDtypeStruct(qkv_weight.shape, BF16),
            jax.ShapeDtypeStruct(out_weight.shape, BF16),
        ),
        in_specs=[hbm] * 5 + [smem] + [hbm] * 2,
        out_specs=(vmem, vmem, vmem),
        scratch_shapes=[
            pltpu.VMEM((parts, 2, 2, depth, block, 256), BF16),
            pltpu.VMEM(fields.shape, BF16),
            pltpu.VMEM(cotangent.shape, BF16),
            pltpu.VMEM((1, tokens), jnp.int32),
            pltpu.VMEM(reward_masks.shape, jnp.int32),
            pltpu.VMEM((1, cat_weight.shape[0]), F32),
            pltpu.VMEM(qkv_weight.shape, BF16),
            pltpu.VMEM(out_weight.shape, BF16),
            dma((7,)),
            pltpu.VMEM((spread, slots, 2 * channels), BF16),
            pltpu.VMEM((2, spread, slots, 2 * channels), BF16),
            pltpu.VMEM((tokens, width), BF16),
            pltpu.VMEM((tokens, width), BF16),
            pltpu.VMEM((spread, slots, channels), BF16),
            pltpu.VMEM((spread, slots, channels), BF16),
            pltpu.VMEM((parts, 2, 2, depth, block, 256), BF16),
            pltpu.VMEM((parts, 2, depth, block, 256), BF16),
            pltpu.VMEM((parts, 2, depth, block, 256), BF16),
            pltpu.VMEM((parts, depth, block, 256), BF16),
            pltpu.VMEM((parts, depth, block, 256), BF16),
            pltpu.VMEM((parts, depth, block, 256), BF16),
            pltpu.VMEM((4, tokens, channels), BF16),
            dma((spread,)), dma((spread,)),
            dma((spread,)), dma((spread,)),
            dma, dma,
            dma((spread,)), dma((spread,)),
            dma((parts,)), dma((parts,)),
            dma((parts,)), dma((parts,)),
            dma((parts, depth)), dma((parts, depth)),
            dma((parts, depth)), dma((parts, depth)),
            dma((parts, depth)), dma((parts, depth)),
            dma((parts, 2, depth)), dma((parts, 2, depth)),
        ],
        compiler_params=pltpu.CompilerParams(
            collective_id=0, has_side_effects=True, vmem_limit_bytes=63 * 1024 * 1024
        ),
        cost_estimate=pl.CostEstimate(
            flops=2_000_000_000, bytes_accessed=8_000_000, transcendentals=300_000
        ),
    )(
        fields,
        cotangent,
        labels.reshape(1, tokens),
        reward_masks,
        cat_weight.reshape(1, -1),
        var_weight,
        qkv_weight,
        out_weight,
    )
    return widen(grad_fields, grad_qkv, grad_out)


def solution(mesh):
    return jax.shard_map(
        shards,
        mesh=mesh,
        in_specs=(
            P(("groups", "tok"), "ch"),
            P(("groups", "tok"), "ch"),
            P(("groups", "tok")),
            P(None, ("groups", "tok")),
            P(),
            P(),
            P(None, None, "ch"),
            P("ch", None),
        ),
        out_specs=(P(("groups", "tok"), "ch"), P("groups", None, "ch"), P(("groups", "ch"), None)),
        check_vma=False,
    )
```

```python
import functools

import jax
import jax.numpy as jnp
from jax import lax
from jax.experimental import pallas as pl
from jax.experimental.pallas import tpu as pltpu
from jax.sharding import PartitionSpec as P

HEAD_DIM = 16
MEMBERS = 64
F32 = jnp.float32
BF16 = jnp.bfloat16
MESH = pl.DeviceIdType.MESH


def nn(a, b):
    return lax.dot_general(a, b, (((1,), (0,)), ((), ())), preferred_element_type=F32)


def nt(a, b):
    return lax.dot_general(a, b, (((1,), (1,)), ((), ())), preferred_element_type=F32)


def tn(a, b):
    return lax.dot_general(a, b, (((0,), (0,)), ((), ())), preferred_element_type=F32)


def iota(shape, dim):
    return lax.broadcasted_iota(jnp.int32, shape, dim)


def repeat(start, stop, body):
    if stop - start <= 8:
        for k in range(start, stop):
            body(k)
    else:
        lax.fori_loop(start, stop, lambda k, _: (body(k), 0)[1], 0)


def spread_matrix(tokens, spread, rows, slots, transposed):
    shape = (tokens, spread * slots) if transposed else (spread * slots, tokens)
    slot, token = (1, 0) if transposed else (0, 1)
    slot, token = iota(shape, slot), iota(shape, token)
    peer, place = slot // slots, slot % slots
    hit = (token == place * spread + peer) & (place < rows)
    return jnp.where(hit, 1.0, 0.0).astype(BF16)


def group_matrix(tokens, spread, rows, slots, transposed):
    shape = (spread * slots, tokens) if transposed else (tokens, spread * slots)
    token, slot = (1, 0) if transposed else (0, 1)
    token, slot = iota(shape, token), iota(shape, slot)
    groups = tokens // MEMBERS
    source = (token % MEMBERS) * groups + token // MEMBERS
    peer, place = slot // slots, slot % slots
    hit = (source == peer * rows + place) & (place < rows)
    return jnp.where(hit, 1.0, 0.0).astype(BF16)


def split_sum(values, ones):
    high = values.astype(BF16)
    low = (values - high.astype(F32)).astype(BF16)
    rows = values.shape[0]
    both = nn(jnp.concatenate([high, low], axis=0), ones)
    return both[:rows] + both[rows:]


def attend(q, k, v, g):
    channels = q.shape[1]
    per = 256 // MEMBERS
    wide = per * MEMBERS
    scale = HEAD_DIM ** (-0.5)
    row_head = iota((wide, channels), 0) // MEMBERS
    col_head = iota((wide, channels), 1) // HEAD_DIM
    ones = iota((wide, wide), 0) // MEMBERS == iota((wide, wide), 1) // MEMBERS
    ones = jnp.where(ones, 1.0, 0.0).astype(BF16)
    k_all = jnp.concatenate([k] * per, axis=0)
    v_all = jnp.concatenate([v] * per, axis=0)
    attended = grad_q = grad_k = grad_v = None
    for chunk in range(channels // HEAD_DIM // per):
        own = row_head + chunk * per == col_head
        keep = jnp.where(own, 1.0, 0.0).astype(BF16)
        k_wide = k_all * keep
        v_wide = v_all * keep
        exponent = jnp.exp(nt(q, k_wide) * scale)
        probs = exponent / split_sum(exponent, ones)
        low = probs.astype(BF16)
        grad_p = nt(g, v_wide)
        grad_scores = probs * (grad_p - split_sum(probs * grad_p, ones))
        grad_low = grad_scores.astype(BF16)
        terms = [nn(low, v_wide), nn(grad_low, k_wide)]
        for left, right in ((grad_low, q), (low, g)):
            full = jnp.where(own, tn(left, right), 0.0)
            part = full[:MEMBERS]
            for h in range(1, per):
                part = part + full[h * MEMBERS:(h + 1) * MEMBERS]
            terms.append(part)
        if chunk == 0:
            attended, grad_q, grad_k, grad_v = terms
        else:
            attended, grad_q = attended + terms[0], grad_q + terms[1]
            grad_k, grad_v = grad_k + terms[2], grad_v + terms[3]
    return (
        attended.astype(BF16),
        (grad_q * scale).astype(BF16),
        (grad_k * scale).astype(BF16),
        grad_v.astype(BF16),
    )


def kernel(
    spread,
    fields_hbm,
    cotangent_hbm,
    labels_hbm,
    masks_hbm,
    cat_weight_hbm,
    var_weight,
    qkv_weight_hbm,
    out_weight_hbm,
    out_fields,
    out_qkv,
    out_out,
    sums,
    fields,
    cotangent,
    labels,
    masks,
    cat_weight,
    qkv_weight,
    out_weight,
    load_sem,
    send,
    got,
    dense_send,
    dense_got,
    back_send,
    back_got,
    terms,
    from_x,
    pair,
    from_w,
    quad,
    from_z,
    stack,
    in_send,
    in_recv,
    fw_send,
    fw_recv,
    de_send,
    de_recv,
    bk_send,
    bk_recv,
    x_send,
    x_recv,
    w_send,
    w_recv,
    z_send,
    z_recv,
    gz_send,
    gz_recv,
    gw_send,
    gw_recv,
    gx_send,
    gx_recv,
):
    loads = [
        pltpu.make_async_copy(source, target, load_sem.at[index])
        for index, (source, target) in enumerate((
            (labels_hbm, labels),
            (cat_weight_hbm, cat_weight),
            (masks_hbm, masks),
            (fields_hbm, fields),
            (cotangent_hbm, cotangent),
            (qkv_weight_hbm, qkv_weight),
            (out_weight_hbm, out_weight),
        ))
    ]
    for load in loads:
        load.start()
    me = lax.axis_index("tok")
    ch = lax.axis_index("ch")
    x, z = lax.rem(me, 2), me // 2
    partner = 2 * z + 1 - x
    zl, zh = lax.rem(z, 2), z // 2
    beside = 2 * (2 * zh + 1 - zl) + x
    tokens, channels = fields.shape
    rows = tokens // spread
    slots = send.shape[1]
    parts, _, _, depth, block, _ = terms.shape

    def remote(src, dst, send_sem, recv_sem, where):
        return pltpu.make_async_remote_copy(
            src_ref=src, dst_ref=dst, send_sem=send_sem, recv_sem=recv_sem,
            device_id=where, device_id_type=MESH,
        )

    barrier = pltpu.get_barrier_semaphore()

    def greet(k):
        pl.semaphore_signal(
            barrier, inc=1, device_id={"tok": lax.rem(me + k, spread)}, device_id_type=MESH
        )

    repeat(1, spread, greet)
    pl.semaphore_signal(barrier, inc=1, device_id={"ch": 1 - ch}, device_id_type=MESH)

    for load in loads[:5]:
        load.wait()
    classes = cat_weight.shape[1]
    onehot = jnp.where(iota((classes, tokens), 0) == labels[...], 1.0, 0.0).astype(BF16)
    left = jnp.broadcast_to(cat_weight[...], (16, classes))
    picked = jnp.zeros((16, tokens), F32)
    for _ in range(3):
        piece = left.astype(BF16)
        picked = picked + nn(piece, onehot)
        left = left - piece.astype(F32)
    boost = jnp.ones((1, tokens), F32)
    seen = masks[...].astype(F32)
    for variable in range(masks.shape[0]):
        boost = boost + var_weight[variable] * seen[variable:variable + 1]
    weight_row = picked[:1] * boost
    diagonal = iota((tokens, tokens), 0) == iota((tokens, tokens), 1)
    weight = jnp.sum(jnp.where(diagonal, weight_row, 0.0), axis=1, keepdims=True)
    weighted = (cotangent[...].astype(F32) * weight).astype(BF16)
    order = spread_matrix(tokens, spread, rows, slots, False)
    send[:, :, :channels] = nn(order, fields[...]).astype(BF16).reshape(spread, slots, channels)
    send[:, :, channels:] = nn(order, weighted).astype(BF16).reshape(spread, slots, channels)

    pl.semaphore_wait(barrier, spread)

    def to_peer(k):
        peer = lax.rem(me + k, spread)
        return remote(
            send.at[peer], got.at[ch, me], in_send.at[peer], in_recv.at[me], {"tok": peer}
        )

    def from_peer(k):
        peer = lax.rem(me + spread - k, spread)
        return peer, remote(
            send.at[peer], got.at[ch, peer], in_send.at[peer], in_recv.at[peer], {"tok": peer}
        )

    def forward(peer):
        return remote(
            got.at[ch, peer], got.at[ch, peer], fw_send.at[peer], fw_recv.at[peer], {"ch": 1 - ch}
        )

    def sibling(peer):
        return remote(
            got.at[1 - ch, peer], got.at[1 - ch, peer], fw_send.at[peer], fw_recv.at[peer],
            {"ch": 1 - ch},
        )

    repeat(1, spread, lambda k: to_peer(k).start())
    got[ch, me] = send[me]
    forward(me).start()

    def pass_on(k):
        peer, copy = from_peer(k)
        copy.wait_recv()
        forward(peer).start()

    repeat(1, spread, pass_on)
    repeat(0, spread, lambda k: sibling(k).wait_recv())

    for load in loads[5:]:
        load.wait()
    place = group_matrix(tokens, spread, rows, slots, False)
    low = nn(place, got[0].reshape(spread * slots, 2 * channels))
    high = nn(place, got[1].reshape(spread * slots, 2 * channels))
    values = jnp.concatenate([low[:, :channels], high[:, :channels]], axis=1)
    grad_full = jnp.concatenate([low[:, channels:], high[:, channels:]], axis=1).astype(BF16)
    centered = values - jnp.mean(values, axis=1, keepdims=True)
    inv_std = lax.rsqrt(jnp.mean(centered * centered, axis=1, keepdims=True) + 1e-05)
    unit = centered * inv_std
    normed = unit.astype(BF16)
    q = nn(normed, qkv_weight[0]).astype(BF16)
    k = nn(normed, qkv_weight[1]).astype(BF16)
    v = nn(normed, qkv_weight[2]).astype(BF16)
    g = nt(grad_full, out_weight[...]).astype(BF16)
    def to_partner(part):
        return remote(
            terms.at[part, 1 - x], from_x.at[part], x_send.at[part], x_recv.at[part],
            {"tok": partner},
        )

    def store_terms(index, value):
        value = value.astype(BF16)
        if parts == 4:
            terms[index] = value.reshape(2, 2, depth, block, 256)
        else:
            terms[0, index // 2, index % 2] = value.reshape(depth, block, 256)

    def part_rows(ref, index):
        if parts == 4:
            return ref[index].reshape(512, 256)
        return ref[0, index // 2, index % 2].reshape(512, 256)

    def to_beside(part):
        return remote(
            pair.at[part, 1 - zl], from_w.at[part], w_send.at[part], w_recv.at[part],
            {"tok": beside},
        )

    def z_peer(step):
        there = lax.rem(zh + step, depth)
        return there, {"tok": 2 * (2 * there + zl) + x}

    def to_z(part, step):
        there, where = z_peer(step)
        return remote(
            quad.at[part, there], from_z.at[part, zh],
            z_send.at[part, there], z_recv.at[part, zh], where,
        )

    def from_z_peer(part, step):
        there, where = z_peer(step)
        return there, remote(
            quad.at[part, there], from_z.at[part, there],
            z_send.at[part, there], z_recv.at[part, there], where,
        )

    def pair_up(part):
        to_partner(part).wait_recv()
        pair[part] = (terms[part, x].astype(F32) + from_x[part].astype(F32)).astype(BF16)
        to_beside(part).start()

    def quad_up(part):
        to_beside(part).wait_recv()
        quad[part] = (pair[part, zl].astype(F32) + from_w[part].astype(F32)).astype(BF16)
        repeat(1, depth, lambda step: to_z(part, step).start())

    turned = normed.astype(F32).T.astype(BF16)
    groups = tokens // MEMBERS
    half = channels // 2
    for h in range(2):
        cols = slice(h * half, (h + 1) * half)
        for group in range(groups):
            rows_of = slice(group * MEMBERS, (group + 1) * MEMBERS)
            results = attend(
                q[rows_of, cols], k[rows_of, cols], v[rows_of, cols], g[rows_of, cols]
            )
            for index, result in enumerate(results):
                stack[index, rows_of, cols] = result
            if h == 1 and parts == 4 and group == groups - 2:
                pair_up(0)
        both = jnp.concatenate([stack[1, :, cols], stack[2, :, cols]], axis=1)
        store_terms(2 * h, nn(turned, both))
        if parts == 4:
            to_partner(2 * h).start()
            if h == 1:
                pair_up(1)
        out_term = tn(stack[0, :, cols], grad_full)
        out_term = jnp.concatenate(
            [out_term[:, j * half:(j + 1) * half] for j in range(4)], axis=0
        )
        value_term = nn(turned, stack[3, :, cols])
        store_terms(2 * h + 1, jnp.concatenate([value_term, out_term], axis=1))
        if parts == 4:
            to_partner(2 * h + 1).start()
    if parts == 1:
        to_partner(0).start()

    dense = nt(stack[1], qkv_weight[0]) + nt(stack[2], qkv_weight[1]) + nt(stack[3], qkv_weight[2])
    dense_send[...] = dense.astype(BF16)
    dense_copy = remote(dense_send, dense_got, de_send, de_recv, {"ch": 1 - ch})
    dense_copy.start()

    if parts == 4:
        quad_up(0)
    else:
        pair_up(0)

    dense_copy.wait()
    dense = dense_send[...].astype(F32) + dense_got[...].astype(F32)
    mean = jnp.mean(dense, axis=1, keepdims=True)
    second = jnp.mean(dense * unit, axis=1, keepdims=True)
    first_half = ch == 0
    own_dense = jnp.where(first_half, dense[:, :channels], dense[:, channels:])
    own_unit = jnp.where(first_half, unit[:, :channels], unit[:, channels:])
    own_grad = jnp.where(first_half, low[:, channels:], high[:, channels:])
    grad = (own_grad + inv_std * (own_dense - mean - own_unit * second)).astype(BF16)
    place_back = group_matrix(tokens, spread, rows, slots, True)
    back_send[...] = nn(place_back, grad).astype(BF16).reshape(spread, slots, channels)

    def give_back(k):
        peer = lax.rem(me + k, spread)
        return remote(
            back_send.at[peer], back_got.at[me], bk_send.at[peer], bk_recv.at[me], {"tok": peer}
        )

    def take_back(k):
        peer = lax.rem(me + spread - k, spread)
        return remote(
            back_send.at[peer], back_got.at[peer], bk_send.at[peer], bk_recv.at[peer],
            {"tok": peer},
        )

    repeat(1, spread, lambda k: give_back(k).start())
    back_got[me] = back_send[me]

    def share_z(part, step):
        there, where = z_peer(step)
        mine = sums.at[part, x, zl, zh]
        return remote(mine, mine, gz_send.at[part, there], gz_recv.at[part, zh], where)

    def shared_z(part, step):
        there, where = z_peer(step)
        other = sums.at[part, x, zl, there]
        return there, remote(
            other, other, gz_send.at[part, there], gz_recv.at[part, there], where
        )

    def share_w(part, there, low_z):
        held = sums.at[part, x, low_z, there]
        return remote(
            held, held, gw_send.at[part, there], gw_recv.at[part, there], {"tok": beside}
        )

    def share_x(part, there, low_z, of_x):
        held = sums.at[part, of_x, low_z, there]
        return remote(
            held, held, gx_send.at[part, low_z, there], gx_recv.at[part, low_z, there],
            {"tok": partner},
        )

    def finish(part):
        if depth <= 9:
            total = quad[part, zh].astype(F32)
            for step in range(1, depth):
                there, copy = from_z_peer(part, step)
                copy.wait_recv()
                total = total + from_z[part, there].astype(F32)
        else:
            def add(step, total):
                there, copy = from_z_peer(part, step)
                copy.wait_recv()
                return total + from_z[part, there].astype(F32)

            total = lax.fori_loop(1, depth, add, quad[part, zh].astype(F32))
        sums[part, x, zl, zh] = total.astype(BF16)
        repeat(1, depth, lambda step: share_z(part, step).start())
        share_w(part, zh, zl).start()
        share_x(part, zh, zl, x).start()

    def go_z(part):
        def go_on(step):
            there, copy = shared_z(part, step)
            copy.wait_recv()
            share_w(part, there, zl).start()
            share_x(part, there, zl, x).start()

        repeat(1, depth, go_on)

    def go_w(part):
        def go_on(step):
            there = lax.rem(zh + step, depth)
            share_w(part, there, 1 - zl).wait_recv()
            share_x(part, there, 1 - zl, x).start()

        repeat(0, depth, go_on)

    def restore():
        repeat(1, spread, lambda k: take_back(k).wait_recv())
        order_back = spread_matrix(tokens, spread, rows, slots, True)
        restored = nn(order_back, back_got[...].reshape(spread * slots, channels))
        out_fields[...] = restored.astype(BF16)

    def place_terms(index):
        block_rows = part_rows(sums, index)
        h = index // 2
        cols = slice(h * half, (h + 1) * half)
        if index % 2 == 0:
            out_qkv[0, :, cols] = block_rows[:, :half]
            out_qkv[1, :, cols] = block_rows[:, half:]
        else:
            out_qkv[2, :, cols] = block_rows[:, :half]
            for j in range(4):
                out_out[cols, j * half:(j + 1) * half] = block_rows[j * half:(j + 1) * half, half:]

    if parts == 4:
        quad_up(1)
        pair_up(2)
        finish(0)
        quad_up(2)
        pair_up(3)
        finish(1)
        go_z(0)
        quad_up(3)
        finish(2)
        go_w(0)
        go_z(1)
        finish(3)
        go_w(1)
        go_z(2)
        restore()
        go_z(3)
        go_w(2)
        go_w(3)
    else:
        quad_up(0)
        finish(0)
        restore()
        go_z(0)
        go_w(0)
    for part in range(parts):
        for low_z in range(2):
            repeat(0, depth, lambda there: share_x(part, there, low_z, 1 - x).wait_recv())
        if parts == 4:
            place_terms(part)
    if parts == 1:
        for index in range(4):
            place_terms(index)

    repeat(1, spread, lambda k: to_peer(k).wait_send())
    repeat(0, spread, lambda k: forward(k).wait_send())
    repeat(1, spread, lambda k: give_back(k).wait_send())
    for part in range(parts):
        to_partner(part).wait_send()
        to_beside(part).wait_send()
        repeat(1, depth, lambda step: to_z(part, step).wait_send())
        repeat(1, depth, lambda step: share_z(part, step).wait_send())
        repeat(0, depth, lambda there: share_w(part, there, zl).wait_send())
        for low_z in range(2):
            repeat(0, depth, lambda there: share_x(part, there, low_z, x).wait_send())


def widen_kernel(fields, qkv, out, fields_wide, qkv_wide, out_wide):
    fields_wide[...] = fields[...]
    qkv_wide[...] = qkv[...].astype(F32)
    out_wide[...] = out[...].astype(F32)


def widen(fields, qkv, out):
    steps = 2
    flat = qkv.reshape(-1, qkv.shape[2])
    arrays = (fields, flat, out)
    specs = [pl.BlockSpec((a.shape[0] // steps, a.shape[1]), lambda i: (i, 0)) for a in arrays]
    fields, flat, out = pl.pallas_call(
        widen_kernel,
        grid=(steps,),
        out_shape=(
            jax.ShapeDtypeStruct(fields.shape, BF16),
            jax.ShapeDtypeStruct(flat.shape, F32),
            jax.ShapeDtypeStruct(out.shape, F32),
        ),
        in_specs=specs,
        out_specs=specs,
        compiler_params=pltpu.CompilerParams(vmem_limit_bytes=63 * 1024 * 1024),
    )(*arrays)
    return fields, flat.reshape(qkv.shape), out


def shards(fields, cotangent, labels, reward_masks, cat_weight, var_weight, qkv_weight, out_weight):
    tokens, channels = fields.shape
    spread = lax.axis_size("tok")
    slots = max(tokens // spread, 16)
    depth = spread // 4
    width = qkv_weight.shape[1]
    total = 2048
    parts = 4 if total // (4 * spread) >= 16 else 1
    block = total // (parts * spread)
    vmem = pl.BlockSpec(memory_space=pltpu.VMEM)
    hbm = pl.BlockSpec(memory_space=pltpu.HBM)
    smem = pl.BlockSpec(memory_space=pltpu.SMEM)
    dma = pltpu.SemaphoreType.DMA
    grad_fields, grad_qkv, grad_out = pl.pallas_call(
        functools.partial(kernel, spread),
        out_shape=(
            jax.ShapeDtypeStruct((tokens, channels), BF16),
            jax.ShapeDtypeStruct(qkv_weight.shape, BF16),
            jax.ShapeDtypeStruct(out_weight.shape, BF16),
        ),
        in_specs=[hbm] * 5 + [smem] + [hbm] * 2,
        out_specs=(vmem, vmem, vmem),
        scratch_shapes=[
            pltpu.VMEM((parts, 2, 2, depth, block, 256), BF16),
            pltpu.VMEM(fields.shape, BF16),
            pltpu.VMEM(cotangent.shape, BF16),
            pltpu.VMEM((1, tokens), jnp.int32),
            pltpu.VMEM(reward_masks.shape, jnp.int32),
            pltpu.VMEM((1, cat_weight.shape[0]), F32),
            pltpu.VMEM(qkv_weight.shape, BF16),
            pltpu.VMEM(out_weight.shape, BF16),
            dma((7,)),
            pltpu.VMEM((spread, slots, 2 * channels), BF16),
            pltpu.VMEM((2, spread, slots, 2 * channels), BF16),
            pltpu.VMEM((tokens, width), BF16),
            pltpu.VMEM((tokens, width), BF16),
            pltpu.VMEM((spread, slots, channels), BF16),
            pltpu.VMEM((spread, slots, channels), BF16),
            pltpu.VMEM((parts, 2, 2, depth, block, 256), BF16),
            pltpu.VMEM((parts, 2, depth, block, 256), BF16),
            pltpu.VMEM((parts, 2, depth, block, 256), BF16),
            pltpu.VMEM((parts, depth, block, 256), BF16),
            pltpu.VMEM((parts, depth, block, 256), BF16),
            pltpu.VMEM((parts, depth, block, 256), BF16),
            pltpu.VMEM((4, tokens, channels), BF16),
            dma((spread,)), dma((spread,)),
            dma((spread,)), dma((spread,)),
            dma, dma,
            dma((spread,)), dma((spread,)),
            dma((parts,)), dma((parts,)),
            dma((parts,)), dma((parts,)),
            dma((parts, depth)), dma((parts, depth)),
            dma((parts, depth)), dma((parts, depth)),
            dma((parts, depth)), dma((parts, depth)),
            dma((parts, 2, depth)), dma((parts, 2, depth)),
        ],
        compiler_params=pltpu.CompilerParams(
            collective_id=0, has_side_effects=True, vmem_limit_bytes=63 * 1024 * 1024
        ),
        cost_estimate=pl.CostEstimate(
            flops=2_000_000_000, bytes_accessed=8_000_000, transcendentals=300_000
        ),
    )(
        fields,
        cotangent,
        labels.reshape(1, tokens),
        reward_masks,
        cat_weight.reshape(1, -1),
        var_weight,
        qkv_weight,
        out_weight,
    )
    return widen(grad_fields, grad_qkv, grad_out)


def solution(mesh):
    return jax.shard_map(
        shards,
        mesh=mesh,
        in_specs=(
            P(("groups", "tok"), "ch"),
            P(("groups", "tok"), "ch"),
            P(("groups", "tok")),
            P(None, ("groups", "tok")),
            P(),
            P(),
            P(None, None, "ch"),
            P("ch", None),
        ),
        out_specs=(P(("groups", "tok"), "ch"), P("groups", None, "ch"), P(("groups", "ch"), None)),
        check_vma=False,
    )
```
